32 devices in a mesh: cuts: 4 (over x, core), tile: 8 (over z, y).
Axes of the slice: x: 2, y: 2, z: 4, core: 2. Of those that a mesh axis runs over, the one named last changes fastest.
Arguments:
- state_in: float32 [4, 2, 128, 1024], P('cuts', None, 'tile'), may hold values from -0.625 to 0.625
- sea_depth: float32 [128, 1024], P('tile'), may hold values from 1.5 to 3
- pressure: float32 [128, 1024], P('tile'), may hold values from -3 to 3
Outputs:
- state_out: float32 [4, 2, 128, 1024], P('cuts', None, 'tile')
The draws below stay inside these ranges and needn't reach their ends.
All inputs are finite; a program needn't handle non-finite values.
Results may differ from the reference program's by a relative error of at most 0.0003.
Values sent between devices are 32-bit elements; how exact they have to be, the bound alone decides.
A program may use at most 64 MiB of HBM per device.

```python
import jax
import jax.numpy as jnp

NY = 1024
LEVELS = 8
DEFECT = 3
SLICES = 4
NX = 128


def draw_sea_depth(key, part):
    across = jnp.arange(NX, dtype=jnp.float32)[:, None] / max(NX - 1, 1)
    incline = 1.8 + 0.8 * across
    roughness = jax.random.uniform(key, (NX, NY), jnp.float32, 0.8, 1.25)
    return jnp.clip(incline * roughness, 1.5, 3.0).astype(jnp.float32)


def level_of(key, extent, shards, least, high):
    def one(dim, shards_of):
        draws = jax.random.uniform(jax.random.fold_in(jax.random.fold_in(key, 6), dim), (shards_of,), jnp.float32, least / len(shards), high / len(shards))
        return jnp.repeat(jnp.exp(draws), extent[dim] // shards_of).reshape((-1,) + (1,) * (len(extent) - dim - 1))

    gain = one(*shards[0])
    for cut in shards[1:]:
        gain = gain * one(*cut)
    return gain


def gaussian(key, shape, spread, reach, pieces=(), kind=jnp.bfloat16):
    gain = level_of(key, shape, pieces, -0.22, 0.18) if pieces else 1.0
    drawn = jax.random.normal(key, shape, jnp.float32) * spread * gain
    return jnp.minimum(jnp.maximum(drawn, -reach), reach).astype(kind)


def setup_inputs(seed: int = 0) -> dict:
    keys = jax.random.split(jax.random.key(seed), 4)
    return {
        "state_in": gaussian(keys[0], (SLICES, 2, NX, NY), 0.25, 0.625, ((0, 4), (2, 8)), jnp.float32),
        "sea_depth": draw_sea_depth(jax.random.fold_in(keys[3], 71), 0),
        "pressure": gaussian(keys[2], (NX, NY), 0.5, 3.0, ((0, 8),), jnp.float32),
    }


TIME_STEP = 0.8
SHIP_SPEED = 0.5
EPSILON = 1e-06

def horizontal(padded):
    middle = padded[..., 1:-1, :]
    widened = jnp.pad(middle, [(0, 0)] * (middle.ndim - 1) + [(1, 1)])
    return padded[..., 2:, :] + padded[..., :-2, :] + widened[..., 2:] + widened[..., :-2] - 4.0 * middle

def vertical_part(potential, surface, vertical):
    above = jnp.concatenate([potential[1:], surface[None]], axis=0)
    below = jnp.concatenate([potential[1:2], potential[:-1]], axis=0)
    return vertical * (above - 2.0 * potential + below)

def operator(padded, surface, vertical):
    return horizontal(padded) + vertical_part(padded[:, 1:-1, :], surface, vertical)

def elimination(vertical):
    diagonal = -2.0 * vertical - 4.0
    inverses = [1.0 / diagonal]
    ratios = [2.0 * vertical * inverses[0]]
    for level in range(1, LEVELS):
        inverse = 1.0 / (diagonal - vertical * ratios[-1])
        inverses.append(inverse)
        ratios.append(vertical * inverse)
    return (inverses, ratios)

def tridiagonal(residual, vertical, factors):
    inverses, ratios = factors
    forward = [residual[0] * inverses[0]]
    for level in range(1, LEVELS):
        forward.append((residual[level] - vertical * forward[-1]) * inverses[level])
    solution = [forward[-1]]
    for level in range(LEVELS - 2, -1, -1):
        solution.append(forward[level] - ratios[level] * solution[-1])
    return jnp.stack(solution[::-1])

def pad_rows(values):
    return jnp.pad(values, ((0, 0), (1, 1), (0, 0)))

def tendency(state, sea_depth, pressure, vertical, factors):
    elevation, potential_top = (state[0], state[1])
    potential = jnp.broadcast_to(potential_top, (LEVELS,) + potential_top.shape)
    residual = -operator(pad_rows(potential), potential_top, vertical)
    flat_zero = jnp.zeros_like(potential_top)
    for sweep in range(DEFECT):
        correction = tridiagonal(residual, vertical, factors)
        image = operator(pad_rows(correction), flat_zero, vertical)
        step_size = jnp.sum(residual * image) / (jnp.sum(image * image) + EPSILON)
        potential = potential + step_size * correction
        if sweep + 1 < DEFECT:
            residual = residual - step_size * image
    vertical_vel = (3.0 * potential_top - 4.0 * potential[-1] + potential[-2]) * LEVELS / (2.0 * sea_depth)
    padded = pad_rows(state)
    east = (padded[:, 2:, :] - padded[:, :-2, :]) * 0.5
    widened = jnp.pad(state, ((0, 0), (0, 0), (1, 1)))
    north = (widened[:, :, 2:] - widened[:, :, :-2]) * 0.5
    slope_sq = east[0] * east[0] + north[0] * north[0]
    height_rate = SHIP_SPEED * east[0] - (east[0] * east[1] + north[0] * north[1]) + vertical_vel * (1.0 + slope_sq)
    flow_rate = SHIP_SPEED * east[1] - elevation - 0.5 * (east[1] * east[1] + north[1] * north[1]) + 0.5 * vertical_vel * vertical_vel * (1.0 + slope_sq) - pressure
    return jnp.stack([height_rate, flow_rate])

def runge_kutta(state, sea_depth, pressure, vertical, factors):
    rate_one = tendency(state, sea_depth, pressure, vertical, factors)
    rate_two = tendency(state + 0.5 * TIME_STEP * rate_one, sea_depth, pressure, vertical, factors)
    rate_three = tendency(state + 0.5 * TIME_STEP * rate_two, sea_depth, pressure, vertical, factors)
    rate_four = tendency(state + TIME_STEP * rate_three, sea_depth, pressure, vertical, factors)
    return state + TIME_STEP / 6.0 * (rate_one + 2.0 * rate_two + 2.0 * rate_three + rate_four)

def coarse_matrix(sea_depth):
    stiffness = jnp.tanh(sea_depth)
    frequency = jnp.sqrt(stiffness)
    cosine = jnp.cos(TIME_STEP * frequency)
    sine_part = jnp.sin(TIME_STEP * frequency)
    return (cosine, stiffness * sine_part / frequency, -sine_part / frequency, cosine)

def coarse_apply(coarse, state):
    return jnp.stack([coarse[0] * state[0] + coarse[1] * state[1], coarse[2] * state[0] + coarse[3] * state[1]])

def reference(state_in, sea_depth, pressure):
    vertical = (LEVELS / sea_depth) ** 2
    factors = elimination(vertical)
    coarse = coarse_matrix(sea_depth)
    defects = []
    for slice_index in range(SLICES):
        fine_state = runge_kutta(state_in[slice_index], sea_depth, pressure, vertical, factors)
        defects.append(fine_state - coarse_apply(coarse, state_in[slice_index]))
    current = state_in[0]
    results = []
    for slice_index in range(SLICES):
        current = coarse_apply(coarse, current) + defects[slice_index]
        results.append(current)
    return jnp.stack(results)
```

```python
import functools
import math

import jax
import jax.numpy as jnp
from jax import lax
from jax.experimental import pallas as pl
from jax.experimental.pallas import tpu as pltpu
from jax.sharding import PartitionSpec as P

LEVELS = 8
STAGES = 4
TIME_STEP = 0.8
SHIP_SPEED = 0.5
EPSILON = 1e-06
MESH = pl.DeviceIdType.MESH
SUB = 8
LANE = 128
REACH = 4
PACK = 8
NSUM = 10

THETA = [(m + 0.5) * math.pi / LEVELS for m in range(LEVELS)]
LAM = [2.0 * math.cos(t) - 2.0 for t in THETA]
WEIGHT = [(-1.0) ** m / math.tan(t / 2) / LEVELS for m, t in enumerate(THETA)]
TOPROW = [
    (math.cos((LEVELS - 2) * t) - 4.0 * math.cos((LEVELS - 1) * t)) * w
    for t, w in zip(THETA, WEIGHT)
]


def masks(shape):
    lane = lax.broadcasted_iota(jnp.int32, shape, len(shape) - 1)
    sub = lax.broadcasted_iota(jnp.int32, shape, len(shape) - 2)
    first = lane == 0
    last = lane == LANE - 1
    return first, first & (sub == 0), last, last & (sub == SUB - 1)


def before(v, mask):
    first, start, _, _ = mask
    r = pltpu.roll(v, 1, axis=2)
    return jnp.where(start, 0.0, jnp.where(first, pltpu.roll(r, 1, axis=1), r))


def after(v, mask):
    _, _, last, end = mask
    r = pltpu.roll(v, LANE - 1, axis=2)
    return jnp.where(end, 0.0, jnp.where(last, pltpu.roll(r, SUB - 1, axis=1), r))


def neighbours(v):
    mid = v[1:-1]
    mask = masks(mid.shape)
    return (v[2:] + v[:-2]) + (before(mid, mask) + after(mid, mask))


def step_sizes(g):
    g00, g01, g02, g03, g11, g12, g13, g22, g23, g33 = g
    gram = [[g00, g01, g02, g03], [g01, g11, g12, g13], [g02, g12, g22, g23], [g03, g13, g23, g33]]

    def quad(c, left, right):
        total = None
        for i, ci in enumerate(c):
            for j, cj in enumerate(c):
                if left == right and j < i:
                    continue
                term = ci * cj * gram[i + left][j + right]
                if left == right and j > i:
                    term = 2.0 * term
                total = term if total is None else total + term
        return total

    coef = [jnp.ones_like(g00)]
    beta = [0.0, 0.0, 0.0]
    for sweep in range(3):
        rr = quad(coef, 0, 0)
        re = quad(coef, 0, 1)
        ee = quad(coef, 1, 1)
        inv = 1.0 / (jnp.maximum(rr + 2.0 * re + ee, 0.0) + EPSILON)
        s = (rr + re) * inv
        t = (re + ee + EPSILON) * inv
        for j, c in enumerate(coef):
            beta[j] = beta[j] + s * c
        nxt = [t * c for c in coef] + [jnp.zeros_like(s)]
        for j, c in enumerate(coef):
            nxt[j + 1] = nxt[j + 1] - s * c
        coef = nxt
    return beta


def kernel(
    tiles, slices, rows, state_ref, depth_ref, press_ref, out_ref,
    st, dep, prs, dm, coarse, first, total, planes, pack, halo, part, slots, chain, chain_in,
    halo_s, halo_r, sum_s, sum_r, chain_s, chain_r,
):
    me = lax.axis_index("tile")
    cut = lax.axis_index("cuts")
    has_lo = me > 0
    has_hi = me < tiles - 1
    has_prev = cut > 0
    has_next = cut < slices - 1
    chunks = [(a, min(4, rows - a)) for a in range(0, rows, 4)]

    halo[...] = jnp.zeros_like(halo)

    barrier = pltpu.get_barrier_semaphore()
    for d in range(1, tiles):
        pl.semaphore_signal(
            barrier, inc=1, device_id={"tile": lax.rem(me + d, tiles)}, device_id_type=MESH
        )

    @pl.when(has_prev)
    def _():
        pl.semaphore_signal(barrier, inc=1, device_id={"cuts": cut - 1}, device_id_type=MESH)

    @pl.when(has_next)
    def _():
        pl.semaphore_signal(barrier, inc=1, device_id={"cuts": cut + 1}, device_id_type=MESH)

    for j in range(SUB):
        cols = slice(j * LANE, (j + 1) * LANE)
        for c in range(2):
            st[c, :, j, :] = state_ref[0, c, :, cols]
        dep[3 : 3 + rows, j, :] = depth_ref[:, cols]
        prs[:, j, :] = press_ref[:, cols]

    first[...] = st[...]

    def halo_copy(s, side, count):
        return pltpu.make_async_remote_copy(
            src_ref=pack.at[s, side, pl.ds(0, count)],
            dst_ref=halo.at[s, 1 - side, pl.ds(0, count)],
            send_sem=halo_s.at[s, side],
            recv_sem=halo_r.at[s, 1 - side],
            device_id={"tile": me - 1 if side == 0 else me + 1},
            device_id_type=MESH,
        )

    def halo_both(s, count, act):
        @pl.when(has_lo)
        def _():
            act(halo_copy, s, 0, count)

        @pl.when(has_hi)
        def _():
            act(halo_copy, s, 1, count)

    start = lambda copy, s, side, count: copy(s, side, count).start()
    arrive = lambda copy, s, side, count: copy(s, 1 - side, count).wait_recv()
    leave = lambda copy, s, side, count: copy(s, side, count).wait_send()

    def fill(s):
        pack[s, 0, 0:4] = st[1, 0:4]
        pack[s, 0, 4:5] = st[0, 0:1]
        pack[s, 1, 0:4] = st[1, rows - 4 : rows]
        pack[s, 1, 4:5] = st[0, rows - 1 : rows]

    fill(0)
    pack[0, 0, 5:8] = dep[3:6]
    pack[0, 1, 5:8] = dep[rows : rows + 3]
    pl.semaphore_wait(
        barrier, tiles - 1 + has_prev.astype(jnp.int32) + has_next.astype(jnp.int32)
    )
    halo_both(0, 8, start)

    own = dep[3 : 3 + rows]
    stiff = jnp.tanh(own)
    z = TIME_STEP * TIME_STEP * stiff
    cosine = 1.0 + z * (-1 / 2 + z * (1 / 24 + z * (-1 / 720 + z * (1 / 40320 - z / 3628800))))
    sine = TIME_STEP * (
        1.0 + z * (-1 / 6 + z * (1 / 120 + z * (-1 / 5040 + z * (1 / 362880 - z / 39916800))))
    )
    coarse[0] = cosine
    coarse[1] = stiff * sine
    coarse[2] = -sine

    halo_both(0, 8, arrive)
    dep[0:3] = halo[0, 0, 5:8]
    dep[rows + 3 : rows + 6] = halo[0, 1, 5:8]
    wide = dep[...]
    row = lax.broadcasted_iota(jnp.int32, wide.shape, 0)
    inside = (has_lo | (row >= 3)) & (has_hi | (row < rows + 3))
    safe = jnp.where(inside, wide, 1.0)
    vert = LEVELS / safe
    vert = vert * vert
    for m in range(LEVELS):
        dm[m] = jnp.where(inside, 1.0 / (vert * LAM[m] - 4.0), 0.0)
    dep[3 : 3 + rows] = (0.5 * LEVELS) / safe[3 : 3 + rows]

    def sum_copy(s, d):
        return pltpu.make_async_remote_copy(
            src_ref=part.at[s],
            dst_ref=slots.at[s, d],
            send_sem=sum_s.at[s, d],
            recv_sem=sum_r.at[s, d],
            device_id={"tile": lax.rem(me + d, tiles)},
            device_id_type=MESH,
        )

    def stage(s, carry):
        lo = halo[s, 0, 0:5]
        hi = halo[s, 1, 0:5]
        top = jnp.concatenate([lo[0:4], st[1], hi[0:4]], axis=0)
        r0 = 4.0 * top[1:-1] - neighbours(top)
        u0 = r0[3:-3]
        gram = [None] * 9
        for m in range(LEVELS):
            c0 = dm[m] * r0
            u1 = neighbours(c0)
            c1 = dm[m, 1:-1] * u1
            u2 = neighbours(c1)
            c2 = dm[m, 2:-2] * u2
            u3 = neighbours(c2)
            us = [u0, u1[2:-2], u2[1:-1], u3]
            cs = [c0[3:-3], c1[2:-2], c2[1:-1]]
            k = 0
            for i in range(4):
                for j in range(max(i, 1), 4):
                    p = (4.0 * WEIGHT[m] ** 2) * jnp.sum(us[i] * us[j], axis=0)
                    gram[k] = p if gram[k] is None else gram[k] + p
                    k += 1
            for i in range(3):
                a = WEIGHT[m] * us[i + 1]
                b = TOPROW[m] * cs[i]
                if m == 0:
                    planes[i] = a
                    planes[3 + i] = b
                else:
                    planes[i] += a
                    planes[3 + i] += b
        bottom = [u0, planes[0], planes[1], planes[2]]
        k = 0
        for i in range(4):
            for j in range(max(i, 1), 4):
                gram[k] = gram[k] + 0.5 * jnp.sum(bottom[i] * bottom[j], axis=0)
                k += 1
        gram = [LEVELS * jnp.sum(u0 * u0, axis=0)] + gram
        for k in range(NSUM):
            part[s, k : k + 1] = jnp.sum(gram[k], axis=0, keepdims=True)
        for k in range(NSUM, 16):
            part[s, k : k + 1] = jnp.zeros((1, LANE), jnp.float32)
        for d in range(1, tiles):
            sum_copy(s, d).start()

        elev = st[0]
        phi = st[1]
        tall = jnp.concatenate([lo[4:5], elev, hi[4:5]], axis=0)
        mask = masks(elev.shape)
        he = 0.5 * (tall[2:] - tall[:-2])
        fe = 0.5 * (top[5:-3] - top[3:-5])
        hn = 0.5 * (after(elev, mask) - before(elev, mask))
        fn = 0.5 * (after(phi, mask) - before(phi, mask))
        slope = 1.0 + he * he + hn * hn
        rate_h = SHIP_SPEED * he - (he * fe + hn * fn)
        rate_f = SHIP_SPEED * fe - elev - 0.5 * (fe * fe + fn * fn) - prs[...]

        for d in range(1, tiles):
            sum_copy(s, d).wait_recv()
        whole = part[s]
        for d in range(1, tiles):
            whole = whole + slots[s, d]
        whole = jnp.sum(whole, axis=1, keepdims=True)
        beta = step_sizes([whole[k : k + 1] for k in range(NSUM)])
        beta = [jnp.broadcast_to(b, (SUB, LANE)) for b in beta]
        w = (beta[0] * planes[3] + beta[1] * planes[4] + beta[2] * planes[5]) * dep[3 : 3 + rows]
        ws = w * slope
        rate_h = rate_h + ws
        rate_f = rate_f + 0.5 * w * ws

        share = jnp.where((s == 0) | (s == STAGES - 1), 1.0, 2.0) * (TIME_STEP / 6.0)
        ahead = jnp.where(s == STAGES - 2, TIME_STEP, 0.5 * TIME_STEP)

        @pl.when(s == 0)
        def _():
            total[...] = first[...]

        total[0] += share * rate_h
        total[1] += share * rate_f
        st[0] = first[0] + ahead * rate_h
        st[1] = first[1] + ahead * rate_f

        @pl.when(s < STAGES - 1)
        def _():
            fill(s + 1)
            halo_both(s + 1, 5, start)
            halo_both(s + 1, 5, arrive)

        return carry

    lax.fori_loop(0, STAGES, stage, 0)

    def chain_copy(k):
        a, size = chunks[k]
        return pltpu.make_async_remote_copy(
            src_ref=chain.at[pl.ds(a, size)],
            dst_ref=chain_in.at[pl.ds(a, size)],
            send_sem=chain_s.at[k],
            recv_sem=chain_r.at[k],
            device_id={"cuts": cut + 1},
            device_id_type=MESH,
        )

    @pl.when(has_prev)
    def _():
        total[0] = total[0] - (coarse[0] * first[0] + coarse[1] * first[1])
        total[1] = total[1] - (coarse[2] * first[0] + coarse[0] * first[1])

    for k, (a, size) in enumerate(chunks):
        span = slice(a, a + size)

        @pl.when(has_prev)
        def _():
            chain_copy(k).wait_recv()
            e = chain_in[span, 0]
            p = chain_in[span, 1]
            chain[span, 0] = coarse[0, span] * e + coarse[1, span] * p + total[0, span]
            chain[span, 1] = coarse[2, span] * e + coarse[0, span] * p + total[1, span]

        @pl.when(jnp.logical_not(has_prev))
        def _():
            chain[span, 0] = total[0, span]
            chain[span, 1] = total[1, span]

        @pl.when(has_next)
        def _():
            chain_copy(k).start()

    for j in range(SUB):
        cols = slice(j * LANE, (j + 1) * LANE)
        for c in range(2):
            out_ref[0, c, :, cols] = chain[:, c, j, :]

    @pl.when(has_next)
    def _():
        for k in range(len(chunks)):
            chain_copy(k).wait_send()

    halo_both(0, 8, leave)
    for s in range(1, STAGES):
        halo_both(s, 5, leave)
    for s in range(STAGES):
        for d in range(1, tiles):
            sum_copy(s, d).wait_send()


def local(tiles, slices, state_in, sea_depth, pressure):
    rows = sea_depth.shape[0]
    plane = (rows, SUB, LANE)
    f32 = jnp.float32
    chunks = -(-rows // 4)
    return pl.pallas_call(
        functools.partial(kernel, tiles, slices, rows),
        out_shape=jax.ShapeDtypeStruct(state_in.shape, f32),
        in_specs=[pl.BlockSpec(memory_space=pltpu.VMEM)] * 3,
        out_specs=pl.BlockSpec(memory_space=pltpu.VMEM),
        scratch_shapes=[
            pltpu.VMEM((2,) + plane, f32),
            pltpu.VMEM((rows + 6, SUB, LANE), f32),
            pltpu.VMEM(plane, f32),
            pltpu.VMEM((LEVELS, rows + 6, SUB, LANE), f32),
            pltpu.VMEM((3,) + plane, f32),
            pltpu.VMEM((2,) + plane, f32),
            pltpu.VMEM((2,) + plane, f32),
            pltpu.VMEM((6,) + plane, f32),
            pltpu.VMEM((STAGES, 2, PACK, SUB, LANE), f32),
            pltpu.VMEM((STAGES, 2, PACK, SUB, LANE), f32),
            pltpu.VMEM((STAGES, 16, LANE), f32),
            pltpu.VMEM((STAGES, tiles, 16, LANE), f32),
            pltpu.VMEM((rows, 2, SUB, LANE), f32),
            pltpu.VMEM((rows, 2, SUB, LANE), f32),
            pltpu.SemaphoreType.DMA((STAGES, 2)),
            pltpu.SemaphoreType.DMA((STAGES, 2)),
            pltpu.SemaphoreType.DMA((STAGES, tiles)),
            pltpu.SemaphoreType.DMA((STAGES, tiles)),
            pltpu.SemaphoreType.DMA((chunks,)),
            pltpu.SemaphoreType.DMA((chunks,)),
        ],
        compiler_params=pltpu.CompilerParams(
            collective_id=0, has_side_effects=True, vmem_limit_bytes=48 * 1024 * 1024
        ),
        name="wake_step",
    )(state_in, sea_depth, pressure)


def solution(mesh):
    placed = (P("cuts", None, "tile", None), P("tile", None), P("tile", None))
    return jax.shard_map(
        functools.partial(local, mesh.shape["tile"], mesh.shape["cuts"]),
        mesh=mesh,
        in_specs=placed,
        out_specs=P("cuts", None, "tile", None),
        check_vma=False,
    )
```

```python
import functools
import math

import jax
import jax.numpy as jnp
from jax import lax
from jax.experimental import pallas as pl
from jax.experimental.pallas import tpu as pltpu
from jax.sharding import PartitionSpec as P

LEVELS = 8
STAGES = 4
TIME_STEP = 0.8
SHIP_SPEED = 0.5
EPSILON = 1e-06
MESH = pl.DeviceIdType.MESH
SUB = 8
LANE = 128
NSUM = 10
FOLD = 5
WIDE = 13
EXTRA = [10, 7, 4, 0]

THETA = [(m + 0.5) * math.pi / LEVELS for m in range(LEVELS)]
LAM = [2.0 * math.cos(t) - 2.0 for t in THETA]
WEIGHT = [(-1.0) ** m / math.tan(t / 2) / LEVELS for m, t in enumerate(THETA)]
TOPROW = [
    (math.cos((LEVELS - 2) * t) - 4.0 * math.cos((LEVELS - 1) * t)) * w
    for t, w in zip(THETA, WEIGHT)
]


def masks(shape):
    lane = lax.broadcasted_iota(jnp.int32, shape, len(shape) - 1)
    sub = lax.broadcasted_iota(jnp.int32, shape, len(shape) - 2)
    first = lane == 0
    last = lane == LANE - 1
    return first, first & (sub == 0), last, last & (sub == SUB - 1)


def before(v, mask):
    first, start, _, _ = mask
    r = pltpu.roll(v, 1, axis=2)
    return jnp.where(start, 0.0, jnp.where(first, pltpu.roll(r, 1, axis=1), r))


def after(v, mask):
    _, _, last, end = mask
    r = pltpu.roll(v, LANE - 1, axis=2)
    return jnp.where(end, 0.0, jnp.where(last, pltpu.roll(r, SUB - 1, axis=1), r))


def neighbours(v):
    mid = v[1:-1]
    mask = masks(mid.shape)
    return (v[2:] + v[:-2]) + (before(mid, mask) + after(mid, mask))


def step_sizes(g):
    g00, g01, g02, g03, g11, g12, g13, g22, g23, g33 = g
    gram = [[g00, g01, g02, g03], [g01, g11, g12, g13], [g02, g12, g22, g23], [g03, g13, g23, g33]]

    def quad(c, left, right):
        total = None
        for i, ci in enumerate(c):
            for j, cj in enumerate(c):
                if left == right and j < i:
                    continue
                term = ci * cj * gram[i + left][j + right]
                if left == right and j > i:
                    term = 2.0 * term
                total = term if total is None else total + term
        return total

    coef = [jnp.ones_like(g00)]
    beta = [0.0, 0.0, 0.0]
    for sweep in range(3):
        rr = quad(coef, 0, 0)
        re = quad(coef, 0, 1)
        ee = quad(coef, 1, 1)
        inv = 1.0 / (jnp.maximum(rr + 2.0 * re + ee, 0.0) + EPSILON)
        s = (rr + re) * inv
        t = (re + ee + EPSILON) * inv
        for j, c in enumerate(coef):
            beta[j] = beta[j] + s * c
        nxt = [t * c for c in coef] + [jnp.zeros_like(s)]
        for j, c in enumerate(coef):
            nxt[j + 1] = nxt[j + 1] - s * c
        coef = nxt
    return beta


def kernel(
    tiles, slices, rows, state_ref, depth_ref, press_ref, out_ref,
    raw, raw_d, raw_p, x, dm, wfac, coarse, first, total, planes, edge, part, slots, chain, chain_in,
    load_s, halo_s, halo_r, sum_s, sum_r, chain_s, chain_r,
):
    me = lax.axis_index("tile")
    cut = lax.axis_index("cuts")
    has_lo = me > 0
    has_hi = me < tiles - 1
    has_prev = cut > 0
    has_next = cut < slices - 1
    chunks = [(a, min(4, rows - a)) for a in range(0, rows, 4)]
    end = WIDE + rows

    loads = [
        pltpu.make_async_copy(state_ref.at[0], raw, load_s.at[0]),
        pltpu.make_async_copy(depth_ref, raw_d, load_s.at[1]),
        pltpu.make_async_copy(press_ref, raw_p, load_s.at[2]),
    ]
    for load in loads:
        load.start()

    x[:, 0:WIDE] = jnp.zeros((4, WIDE, SUB, LANE), jnp.float32)
    x[:, end : end + WIDE] = jnp.zeros((4, WIDE, SUB, LANE), jnp.float32)

    barrier = pltpu.get_barrier_semaphore()
    for d in range(1, tiles):
        pl.semaphore_signal(
            barrier, inc=1, device_id={"tile": lax.rem(me + d, tiles)}, device_id_type=MESH
        )

    @pl.when(has_prev)
    def _():
        pl.semaphore_signal(barrier, inc=1, device_id={"cuts": cut - 1}, device_id_type=MESH)

    @pl.when(has_next)
    def _():
        pl.semaphore_signal(barrier, inc=1, device_id={"cuts": cut + 1}, device_id_type=MESH)

    for load in loads:
        load.wait()
    for j in range(SUB):
        cols = slice(j * LANE, (j + 1) * LANE)
        x[0, WIDE:end, j, :] = raw[1, :, cols]
        x[1, WIDE:end, j, :] = raw_d[:, cols]
        x[2, WIDE:end, j, :] = raw[0, :, cols]
        x[3, WIDE:end, j, :] = raw_p[:, cols]

    parts = [(0, 2, 0, 4), (0, 2, 4, WIDE - 4), (2, 2, 0, WIDE - 2)]

    def halo_copy(k, side):
        p, np_, a, size = parts[k]
        if side == 0:
            src, dst = WIDE + a, end + a
        else:
            src, dst = end - a - size, WIDE - a - size
        return pltpu.make_async_remote_copy(
            src_ref=x.at[pl.ds(p, np_), pl.ds(src, size)],
            dst_ref=x.at[pl.ds(p, np_), pl.ds(dst, size)],
            send_sem=halo_s.at[k, side],
            recv_sem=halo_r.at[k, side],
            device_id={"tile": me - 1 if side == 0 else me + 1},
            device_id_type=MESH,
        )

    def halo_both(k, act):
        @pl.when(has_lo)
        def _():
            act(k, 0)

        @pl.when(has_hi)
        def _():
            act(k, 1)

    start = lambda k, side: halo_copy(k, side).start()
    arrive = lambda k, side: halo_copy(k, 1 - side).wait_recv()
    leave = lambda k, side: halo_copy(k, side).wait_send()

    def columns(a, b, inside):
        safe = x[1, a:b]
        if inside is not None:
            safe = jnp.where(inside, safe, 1.0)
        vert = LEVELS / safe
        vert = vert * vert
        for m in range(LEVELS):
            inverse = 1.0 / (vert * LAM[m] - 4.0)
            dm[m, a:b] = inverse if inside is None else jnp.where(inside, inverse, 0.0)
        wfac[a:b] = (0.5 * LEVELS) / safe

    pl.semaphore_wait(
        barrier, tiles - 1 + has_prev.astype(jnp.int32) + has_next.astype(jnp.int32)
    )
    for k in range(3):
        halo_both(k, start)

    columns(WIDE, end, None)
    own = x[1, WIDE:end]
    stiff = jnp.tanh(own)
    z = TIME_STEP * TIME_STEP * stiff
    cosine = 1.0 + z * (-1 / 2 + z * (1 / 24 + z * (-1 / 720 + z * (1 / 40320 - z / 3628800))))
    sine = TIME_STEP * (
        1.0 + z * (-1 / 6 + z * (1 / 120 + z * (-1 / 5040 + z * (1 / 362880 - z / 39916800))))
    )
    coarse[0] = cosine
    coarse[1] = stiff * sine
    coarse[2] = -sine

    halo_both(0, arrive)
    columns(WIDE - 3, WIDE, has_lo)
    columns(end, end + 3, has_hi)

    def sum_copy(s, d):
        return pltpu.make_async_remote_copy(
            src_ref=part.at[s],
            dst_ref=slots.at[s, d],
            send_sem=sum_s.at[s, d],
            recv_sem=sum_r.at[s, d],
            device_id={"tile": lax.rem(me + d, tiles)},
            device_id_type=MESH,
        )

    half = lax.broadcasted_iota(jnp.int32, (1, LANE), 1) < LANE // 2

    def inner_products(s):
        top = x[0, WIDE - 4 : end + 4]
        r0 = 4.0 * top[1:-1] - neighbours(top)
        u0 = r0[3:-3]
        gram = [None] * 9
        for m in range(LEVELS):
            c0 = dm[m, WIDE - 3 : end + 3] * r0
            u1 = neighbours(c0)
            c1 = dm[m, WIDE - 2 : end + 2] * u1
            u2 = neighbours(c1)
            c2 = dm[m, WIDE - 1 : end + 1] * u2
            u3 = neighbours(c2)
            us = [u0, u1[2:-2], u2[1:-1], u3]
            cs = [c0[3:-3], c1[2:-2], c2[1:-1]]
            k = 0
            for i in range(4):
                for j in range(max(i, 1), 4):
                    p = (4.0 * WEIGHT[m] ** 2) * jnp.sum(us[i] * us[j], axis=0)
                    gram[k] = p if gram[k] is None else gram[k] + p
                    k += 1
            for i in range(3):
                a = WEIGHT[m] * us[i + 1]
                b = TOPROW[m] * cs[i]
                if m == 0:
                    planes[i] = a
                    planes[3 + i] = b
                else:
                    planes[i] += a
                    planes[3 + i] += b
        bottom = [u0, planes[0], planes[1], planes[2]]
        k = 0
        for i in range(4):
            for j in range(max(i, 1), 4):
                gram[k] = gram[k] + 0.5 * jnp.sum(bottom[i] * bottom[j], axis=0)
                k += 1
        gram = [LEVELS * jnp.sum(u0 * u0, axis=0)] + gram
        gram = [jnp.sum(g, axis=0, keepdims=True) for g in gram]
        for k in range(FOLD):
            a, b = gram[k], gram[k + FOLD]
            part[s, k : k + 1] = jnp.where(half, a, b) + pltpu.roll(
                jnp.where(half, b, a), LANE // 2, axis=1
            )

    def beyond(side, a, b):
        top = x[0, a - 3 : b + 3]
        r0 = 4.0 * top[1:-1] - neighbours(top)
        size = b - a
        for m in range(LEVELS):
            c0 = dm[m, a - 2 : b + 2] * r0
            c1 = dm[m, a - 1 : b + 1] * neighbours(c0)
            c2 = dm[m, a:b] * neighbours(c1)
            for i, c in enumerate([c0[2:-2], c1[1:-1], c2]):
                v = TOPROW[m] * c
                if m == 0:
                    edge[side, i, 0:size] = v
                else:
                    edge[side, i, 0:size] += v

    def explicit(a, b):
        elev = x[2, a:b]
        phi = x[0, a:b]
        mask = masks(elev.shape)
        he = 0.5 * (x[2, a + 1 : b + 1] - x[2, a - 1 : b - 1])
        fe = 0.5 * (x[0, a + 1 : b + 1] - x[0, a - 1 : b - 1])
        hn = 0.5 * (after(elev, mask) - before(elev, mask))
        fn = 0.5 * (after(phi, mask) - before(phi, mask))
        slope = 1.0 + he * he + hn * hn
        rate_h = SHIP_SPEED * he - (he * fe + hn * fn)
        rate_f = SHIP_SPEED * fe - elev - 0.5 * (fe * fe + fn * fn) - x[3, a:b]
        return slope, rate_h, rate_f

    for s in range(STAGES):
        extra = EXTRA[s]
        inner_products(s)
        for d in range(1, tiles):
            sum_copy(s, d).start()

        if s == 0:
            halo_both(1, arrive)
            halo_both(2, arrive)
            columns(1, WIDE - 3, has_lo)
            columns(end + 3, end + WIDE - 1, has_hi)
            first[0] = x[2]
            first[1] = x[0]
        regions = [(WIDE, end, None)]
        if extra:
            beyond(0, WIDE - extra, WIDE)
            beyond(1, end, end + extra)
            regions += [(WIDE - extra, WIDE, 0), (end, end + extra, 1)]
        known = [explicit(a, b) for a, b, _ in regions]
        if s == 0:
            for k in range(3):
                halo_both(k, leave)

        for d in range(1, tiles):
            sum_copy(s, d).wait_recv()
        whole = part[s]
        for d in range(1, tiles):
            whole = whole + slots[s, d]
        low = jnp.sum(jnp.where(half, whole, 0.0), axis=1, keepdims=True)
        high = jnp.sum(jnp.where(half, 0.0, whole), axis=1, keepdims=True)
        sums = [low[k : k + 1] for k in range(FOLD)] + [high[k : k + 1] for k in range(FOLD)]
        beta = [jnp.broadcast_to(b, (SUB, LANE)) for b in step_sizes(sums)]

        share = (1.0 if s in (0, STAGES - 1) else 2.0) * (TIME_STEP / 6.0)
        ahead = TIME_STEP if s == STAGES - 2 else 0.5 * TIME_STEP
        for (a, b, side), (slope, rate_h, rate_f) in zip(regions, known):
            if side is None:
                y = [planes[3 + i] for i in range(3)]
            else:
                y = [edge[side, i, 0 : b - a] for i in range(3)]
            w = (beta[0] * y[0] + beta[1] * y[1] + beta[2] * y[2]) * wfac[a:b]
            ws = w * slope
            rate_h = rate_h + ws
            rate_f = rate_f + 0.5 * w * ws
            if side is None:
                if s == 0:
                    total[0] = first[0, a:b] + share * rate_h
                    total[1] = first[1, a:b] + share * rate_f
                else:
                    total[0] += share * rate_h
                    total[1] += share * rate_f
            if s < STAGES - 1:
                new_h = first[0, a:b] + ahead * rate_h
                new_f = first[1, a:b] + ahead * rate_f
                if side is not None:
                    there = has_hi if side else has_lo
                    new_h = jnp.where(there, new_h, 0.0)
                    new_f = jnp.where(there, new_f, 0.0)
                x[2, a:b] = new_h
                x[0, a:b] = new_f

    def chain_copy(k):
        a, size = chunks[k]
        return pltpu.make_async_remote_copy(
            src_ref=chain.at[pl.ds(a, size)],
            dst_ref=chain_in.at[pl.ds(a, size)],
            send_sem=chain_s.at[k],
            recv_sem=chain_r.at[k],
            device_id={"cuts": cut + 1},
            device_id_type=MESH,
        )

    @pl.when(has_prev)
    def _():
        e = first[0, WIDE:end]
        p = first[1, WIDE:end]
        total[0] = total[0] - (coarse[0] * e + coarse[1] * p)
        total[1] = total[1] - (coarse[2] * e + coarse[0] * p)

    for k, (a, size) in enumerate(chunks):
        span = slice(a, a + size)

        @pl.when(has_prev)
        def _():
            chain_copy(k).wait_recv()
            e = chain_in[span, 0]
            p = chain_in[span, 1]
            chain[span, 0] = coarse[0, span] * e + coarse[1, span] * p + total[0, span]
            chain[span, 1] = coarse[2, span] * e + coarse[0, span] * p + total[1, span]

        @pl.when(jnp.logical_not(has_prev))
        def _():
            chain[span, 0] = total[0, span]
            chain[span, 1] = total[1, span]

        @pl.when(has_next)
        def _():
            chain_copy(k).start()

    for j in range(SUB):
        cols = slice(j * LANE, (j + 1) * LANE)
        for c in range(2):
            out_ref[0, c, :, cols] = chain[:, c, j, :]

    @pl.when(has_next)
    def _():
        for k in range(len(chunks)):
            chain_copy(k).wait_send()

    for s in range(STAGES):
        for d in range(1, tiles):
            sum_copy(s, d).wait_send()


def local(tiles, slices, state_in, sea_depth, pressure):
    rows = sea_depth.shape[0]
    plane = (rows, SUB, LANE)
    wide = rows + 2 * WIDE
    f32 = jnp.float32
    chunks = -(-rows // 4)
    return pl.pallas_call(
        functools.partial(kernel, tiles, slices, rows),
        out_shape=jax.ShapeDtypeStruct(state_in.shape, f32),
        in_specs=[pl.BlockSpec(memory_space=pltpu.HBM)] * 3,
        out_specs=pl.BlockSpec(memory_space=pltpu.VMEM),
        scratch_shapes=[
            pltpu.VMEM(state_in.shape[1:], f32),
            pltpu.VMEM(sea_depth.shape, f32),
            pltpu.VMEM(pressure.shape, f32),
            pltpu.VMEM((4, wide, SUB, LANE), f32),
            pltpu.VMEM((LEVELS, wide, SUB, LANE), f32),
            pltpu.VMEM((wide, SUB, LANE), f32),
            pltpu.VMEM((3,) + plane, f32),
            pltpu.VMEM((2, wide, SUB, LANE), f32),
            pltpu.VMEM((2,) + plane, f32),
            pltpu.VMEM((6,) + plane, f32),
            pltpu.VMEM((2, 3, EXTRA[0], SUB, LANE), f32),
            pltpu.VMEM((STAGES, FOLD, LANE), f32),
            pltpu.VMEM((STAGES, tiles, FOLD, LANE), f32),
            pltpu.VMEM((rows, 2, SUB, LANE), f32),
            pltpu.VMEM((rows, 2, SUB, LANE), f32),
            pltpu.SemaphoreType.DMA((3,)),
            pltpu.SemaphoreType.DMA((3, 2)),
            pltpu.SemaphoreType.DMA((3, 2)),
            pltpu.SemaphoreType.DMA((STAGES, tiles)),
            pltpu.SemaphoreType.DMA((STAGES, tiles)),
            pltpu.SemaphoreType.DMA((chunks,)),
            pltpu.SemaphoreType.DMA((chunks,)),
        ],
        compiler_params=pltpu.CompilerParams(
            collective_id=0, has_side_effects=True, vmem_limit_bytes=48 * 1024 * 1024
        ),
        name="wake_step",
    )(state_in, sea_depth, pressure)


def solution(mesh):
    placed = (P("cuts", None, "tile", None), P("tile", None), P("tile", None))
    return jax.shard_map(
        functools.partial(local, mesh.shape["tile"], mesh.shape["cuts"]),
        mesh=mesh,
        in_specs=placed,
        out_specs=P("cuts", None, "tile", None),
        check_vma=False,
    )
```

```python
import functools
import math

import jax
import jax.numpy as jnp
from jax import lax
from jax.experimental import pallas as pl
from jax.experimental.pallas import tpu as pltpu
from jax.sharding import PartitionSpec as P

LEVELS = 8
STAGES = 4
TIME_STEP = 0.8
SHIP_SPEED = 0.5
EPSILON = 1e-06
MESH = pl.DeviceIdType.MESH
SUB = 8
LANE = 128
NSUM = 10
FOLD = 5
WIDE = 13
EXTRA = [10, 7, 4, 0]

THETA = [(m + 0.5) * math.pi / LEVELS for m in range(LEVELS)]
LAM = [2.0 * math.cos(t) - 2.0 for t in THETA]
WEIGHT = [(-1.0) ** m / math.tan(t / 2) / LEVELS for m, t in enumerate(THETA)]
TOPROW = [
    (math.cos((LEVELS - 2) * t) - 4.0 * math.cos((LEVELS - 1) * t)) * w
    for t, w in zip(THETA, WEIGHT)
]


def masks(shape):
    lane = lax.broadcasted_iota(jnp.int32, shape, len(shape) - 1)
    sub = lax.broadcasted_iota(jnp.int32, shape, len(shape) - 2)
    first = lane == 0
    last = lane == LANE - 1
    return first, first & (sub == 0), last, last & (sub == SUB - 1)


def before(v, mask):
    first, start, _, _ = mask
    r = pltpu.roll(v, 1, axis=2)
    return jnp.where(start, 0.0, jnp.where(first, pltpu.roll(r, 1, axis=1), r))


def after(v, mask):
    _, _, last, end = mask
    r = pltpu.roll(v, LANE - 1, axis=2)
    return jnp.where(end, 0.0, jnp.where(last, pltpu.roll(r, SUB - 1, axis=1), r))


def neighbours(v):
    mid = v[1:-1]
    mask = masks(mid.shape)
    return (v[2:] + v[:-2]) + (before(mid, mask) + after(mid, mask))


def step_sizes(g):
    g00, g01, g02, g03, g11, g12, g13, g22, g23, g33 = g
    gram = [[g00, g01, g02, g03], [g01, g11, g12, g13], [g02, g12, g22, g23], [g03, g13, g23, g33]]

    def quad(c, left, right):
        total = None
        for i, ci in enumerate(c):
            for j, cj in enumerate(c):
                if left == right and j < i:
                    continue
                term = ci * cj * gram[i + left][j + right]
                if left == right and j > i:
                    term = 2.0 * term
                total = term if total is None else total + term
        return total

    coef = [jnp.ones_like(g00)]
    beta = [0.0, 0.0, 0.0]
    for sweep in range(3):
        rr = quad(coef, 0, 0)
        re = quad(coef, 0, 1)
        ee = quad(coef, 1, 1)
        inv = 1.0 / (jnp.maximum(rr + 2.0 * re + ee, 0.0) + EPSILON)
        s = (rr + re) * inv
        t = (re + ee + EPSILON) * inv
        for j, c in enumerate(coef):
            beta[j] = beta[j] + s * c
        nxt = [t * c for c in coef] + [jnp.zeros_like(s)]
        for j, c in enumerate(coef):
            nxt[j + 1] = nxt[j + 1] - s * c
        coef = nxt
    return beta


def kernel(
    tiles, slices, rows, state_ref, depth_ref, press_ref, out_ref,
    raw, raw_d, raw_p, x, dm, wfac, coarse, first, total, planes, edge, part, slots, chain, chain_in,
    load_s, halo_s, halo_r, sum_s, sum_r, chain_s, chain_r,
):
    me = lax.axis_index("tile")
    cut = lax.axis_index("cuts")
    has_lo = me > 0
    has_hi = me < tiles - 1
    has_prev = cut > 0
    has_next = cut < slices - 1
    chunks = [(a, min(4, rows - a)) for a in range(0, rows, 4)]
    end = WIDE + rows

    loads = [
        pltpu.make_async_copy(state_ref.at[0], raw, load_s.at[0]),
        pltpu.make_async_copy(depth_ref, raw_d, load_s.at[1]),
        pltpu.make_async_copy(press_ref, raw_p, load_s.at[2]),
    ]
    for load in loads:
        load.start()

    x[:, 0:WIDE] = jnp.zeros((4, WIDE, SUB, LANE), jnp.float32)
    x[:, end : end + WIDE] = jnp.zeros((4, WIDE, SUB, LANE), jnp.float32)

    barrier = pltpu.get_barrier_semaphore()
    for d in range(1, tiles):
        pl.semaphore_signal(
            barrier, inc=1, device_id={"tile": lax.rem(me + d, tiles)}, device_id_type=MESH
        )

    @pl.when(has_prev)
    def _():
        pl.semaphore_signal(barrier, inc=1, device_id={"cuts": cut - 1}, device_id_type=MESH)

    @pl.when(has_next)
    def _():
        pl.semaphore_signal(barrier, inc=1, device_id={"cuts": cut + 1}, device_id_type=MESH)

    for load in loads:
        load.wait()
    for j in range(SUB):
        cols = slice(j * LANE, (j + 1) * LANE)
        x[0, WIDE:end, j, :] = raw[1, :, cols]
        x[1, WIDE:end, j, :] = raw_d[:, cols]
        x[2, WIDE:end, j, :] = raw[0, :, cols]
        x[3, WIDE:end, j, :] = raw_p[:, cols]

    parts = [(0, 2, 0, 4), (0, 2, 4, WIDE - 4), (2, 2, 0, WIDE - 2)]

    def halo_copy(k, side):
        p, np_, a, size = parts[k]
        if side == 0:
            src, dst = WIDE + a, end + a
        else:
            src, dst = end - a - size, WIDE - a - size
        return pltpu.make_async_remote_copy(
            src_ref=x.at[pl.ds(p, np_), pl.ds(src, size)],
            dst_ref=x.at[pl.ds(p, np_), pl.ds(dst, size)],
            send_sem=halo_s.at[k, side],
            recv_sem=halo_r.at[k, side],
            device_id={"tile": me - 1 if side == 0 else me + 1},
            device_id_type=MESH,
        )

    def halo_both(k, act):
        @pl.when(has_lo)
        def _():
            act(k, 0)

        @pl.when(has_hi)
        def _():
            act(k, 1)

    start = lambda k, side: halo_copy(k, side).start()
    arrive = lambda k, side: halo_copy(k, 1 - side).wait_recv()
    leave = lambda k, side: halo_copy(k, side).wait_send()

    def columns(a, b, inside):
        safe = x[1, a:b]
        if inside is not None:
            safe = jnp.where(inside, safe, 1.0)
        vert = LEVELS / safe
        vert = vert * vert
        for m in range(LEVELS):
            inverse = 1.0 / (vert * LAM[m] - 4.0)
            dm[m, a:b] = inverse if inside is None else jnp.where(inside, inverse, 0.0)
        wfac[a:b] = (0.5 * LEVELS) / safe

    columns(WIDE, end, None)
    own = x[1, WIDE:end]
    stiff = jnp.tanh(own)
    z = TIME_STEP * TIME_STEP * stiff
    cosine = 1.0 + z * (-1 / 2 + z * (1 / 24 + z * (-1 / 720 + z * (1 / 40320 - z / 3628800))))
    sine = TIME_STEP * (
        1.0 + z * (-1 / 6 + z * (1 / 120 + z * (-1 / 5040 + z * (1 / 362880 - z / 39916800))))
    )
    coarse[0] = cosine
    coarse[1] = stiff * sine
    coarse[2] = -sine

    pl.semaphore_wait(
        barrier, tiles - 1 + has_prev.astype(jnp.int32) + has_next.astype(jnp.int32)
    )
    for k in range(3):
        halo_both(k, start)

    halo_both(0, arrive)
    columns(WIDE - 3, WIDE, has_lo)
    columns(end, end + 3, has_hi)

    def sum_copy(s, d):
        return pltpu.make_async_remote_copy(
            src_ref=part.at[s],
            dst_ref=slots.at[s, d],
            send_sem=sum_s.at[s, d],
            recv_sem=sum_r.at[s, d],
            device_id={"tile": lax.rem(me + d, tiles)},
            device_id_type=MESH,
        )

    half = lax.broadcasted_iota(jnp.int32, (1, LANE), 1) < LANE // 2

    def inner_products(s):
        top = x[0, WIDE - 4 : end + 4]
        r0 = 4.0 * top[1:-1] - neighbours(top)
        u0 = r0[3:-3]
        gram = [None] * 9
        for m in range(LEVELS):
            c0 = dm[m, WIDE - 3 : end + 3] * r0
            u1 = neighbours(c0)
            c1 = dm[m, WIDE - 2 : end + 2] * u1
            u2 = neighbours(c1)
            c2 = dm[m, WIDE - 1 : end + 1] * u2
            u3 = neighbours(c2)
            us = [u0, u1[2:-2], u2[1:-1], u3]
            cs = [c0[3:-3], c1[2:-2], c2[1:-1]]
            k = 0
            for i in range(4):
                for j in range(max(i, 1), 4):
                    p = (4.0 * WEIGHT[m] ** 2) * jnp.sum(us[i] * us[j], axis=0)
                    gram[k] = p if gram[k] is None else gram[k] + p
                    k += 1
            for i in range(3):
                a = WEIGHT[m] * us[i + 1]
                b = TOPROW[m] * cs[i]
                if m == 0:
                    planes[i] = a
                    planes[3 + i] = b
                else:
                    planes[i] += a
                    planes[3 + i] += b
        bottom = [u0, planes[0], planes[1], planes[2]]
        k = 0
        for i in range(4):
            for j in range(max(i, 1), 4):
                gram[k] = gram[k] + 0.5 * jnp.sum(bottom[i] * bottom[j], axis=0)
                k += 1
        gram = [LEVELS * jnp.sum(u0 * u0, axis=0)] + gram
        gram = [jnp.sum(g, axis=0, keepdims=True) for g in gram]
        for k in range(FOLD):
            a, b = gram[k], gram[k + FOLD]
            part[s, k : k + 1] = jnp.where(half, a, b) + pltpu.roll(
                jnp.where(half, b, a), LANE // 2, axis=1
            )

    def beyond(side, a, b):
        top = x[0, a - 3 : b + 3]
        r0 = 4.0 * top[1:-1] - neighbours(top)
        size = b - a
        for m in range(LEVELS):
            c0 = dm[m, a - 2 : b + 2] * r0
            c1 = dm[m, a - 1 : b + 1] * neighbours(c0)
            c2 = dm[m, a:b] * neighbours(c1)
            for i, c in enumerate([c0[2:-2], c1[1:-1], c2]):
                v = TOPROW[m] * c
                if m == 0:
                    edge[side, i, 0:size] = v
                else:
                    edge[side, i, 0:size] += v

    def explicit(a, b):
        elev = x[2, a:b]
        phi = x[0, a:b]
        mask = masks(elev.shape)
        he = 0.5 * (x[2, a + 1 : b + 1] - x[2, a - 1 : b - 1])
        fe = 0.5 * (x[0, a + 1 : b + 1] - x[0, a - 1 : b - 1])
        hn = 0.5 * (after(elev, mask) - before(elev, mask))
        fn = 0.5 * (after(phi, mask) - before(phi, mask))
        slope = 1.0 + he * he + hn * hn
        rate_h = SHIP_SPEED * he - (he * fe + hn * fn)
        rate_f = SHIP_SPEED * fe - elev - 0.5 * (fe * fe + fn * fn) - x[3, a:b]
        return slope, rate_h, rate_f

    for s in range(STAGES):
        extra = EXTRA[s]
        inner_products(s)
        for d in range(1, tiles):
            sum_copy(s, d).start()

        if s == 0:
            halo_both(1, arrive)
            halo_both(2, arrive)
            columns(1, WIDE - 3, has_lo)
            columns(end + 3, end + WIDE - 1, has_hi)
            first[0] = x[2]
            first[1] = x[0]
        regions = [(WIDE, end, None)]
        if extra:
            beyond(0, WIDE - extra, WIDE)
            beyond(1, end, end + extra)
            regions += [(WIDE - extra, WIDE, 0), (end, end + extra, 1)]
        known = [explicit(a, b) for a, b, _ in regions]
        if s == 0:
            for k in range(3):
                halo_both(k, leave)

        for d in range(1, tiles):
            sum_copy(s, d).wait_recv()
        whole = part[s]
        for d in range(1, tiles):
            whole = whole + slots[s, d]
        low = jnp.sum(jnp.where(half, whole, 0.0), axis=1, keepdims=True)
        high = jnp.sum(jnp.where(half, 0.0, whole), axis=1, keepdims=True)
        sums = [low[k : k + 1] for k in range(FOLD)] + [high[k : k + 1] for k in range(FOLD)]
        beta = [jnp.broadcast_to(b, (SUB, LANE)) for b in step_sizes(sums)]

        share = (1.0 if s in (0, STAGES - 1) else 2.0) * (TIME_STEP / 6.0)
        ahead = TIME_STEP if s == STAGES - 2 else 0.5 * TIME_STEP
        for (a, b, side), (slope, rate_h, rate_f) in zip(regions, known):
            if side is None:
                y = [planes[3 + i] for i in range(3)]
            else:
                y = [edge[side, i, 0 : b - a] for i in range(3)]
            w = (beta[0] * y[0] + beta[1] * y[1] + beta[2] * y[2]) * wfac[a:b]
            ws = w * slope
            rate_h = rate_h + ws
            rate_f = rate_f + 0.5 * w * ws
            if side is None:
                if s == 0:
                    total[0] = first[0, a:b] + share * rate_h
                    total[1] = first[1, a:b] + share * rate_f
                else:
                    total[0] += share * rate_h
                    total[1] += share * rate_f
            if s < STAGES - 1:
                new_h = first[0, a:b] + ahead * rate_h
                new_f = first[1, a:b] + ahead * rate_f
                if side is not None:
                    there = has_hi if side else has_lo
                    new_h = jnp.where(there, new_h, 0.0)
                    new_f = jnp.where(there, new_f, 0.0)
                x[2, a:b] = new_h
                x[0, a:b] = new_f

    def chain_copy(k):
        a, size = chunks[k]
        return pltpu.make_async_remote_copy(
            src_ref=chain.at[pl.ds(a, size)],
            dst_ref=chain_in.at[pl.ds(a, size)],
            send_sem=chain_s.at[k],
            recv_sem=chain_r.at[k],
            device_id={"cuts": cut + 1},
            device_id_type=MESH,
        )

    @pl.when(has_prev)
    def _():
        e = first[0, WIDE:end]
        p = first[1, WIDE:end]
        total[0] = total[0] - (coarse[0] * e + coarse[1] * p)
        total[1] = total[1] - (coarse[2] * e + coarse[0] * p)

    for k, (a, size) in enumerate(chunks):
        span = slice(a, a + size)

        @pl.when(has_prev)
        def _():
            chain_copy(k).wait_recv()
            e = chain_in[span, 0]
            p = chain_in[span, 1]
            chain[span, 0] = coarse[0, span] * e + coarse[1, span] * p + total[0, span]
            chain[span, 1] = coarse[2, span] * e + coarse[0, span] * p + total[1, span]

        @pl.when(jnp.logical_not(has_prev))
        def _():
            chain[span, 0] = total[0, span]
            chain[span, 1] = total[1, span]

        @pl.when(has_next)
        def _():
            chain_copy(k).start()

    for j in range(SUB):
        cols = slice(j * LANE, (j + 1) * LANE)
        for c in range(2):
            out_ref[0, c, :, cols] = chain[:, c, j, :]

    @pl.when(has_next)
    def _():
        for k in range(len(chunks)):
            chain_copy(k).wait_send()

    for s in range(STAGES):
        for d in range(1, tiles):
            sum_copy(s, d).wait_send()


def local(tiles, slices, state_in, sea_depth, pressure):
    rows = sea_depth.shape[0]
    plane = (rows, SUB, LANE)
    wide = rows + 2 * WIDE
    f32 = jnp.float32
    chunks = -(-rows // 4)
    return pl.pallas_call(
        functools.partial(kernel, tiles, slices, rows),
        out_shape=jax.ShapeDtypeStruct(state_in.shape, f32),
        in_specs=[pl.BlockSpec(memory_space=pltpu.HBM)] * 3,
        out_specs=pl.BlockSpec(memory_space=pltpu.VMEM),
        scratch_shapes=[
            pltpu.VMEM(state_in.shape[1:], f32),
            pltpu.VMEM(sea_depth.shape, f32),
            pltpu.VMEM(pressure.shape, f32),
            pltpu.VMEM((4, wide, SUB, LANE), f32),
            pltpu.VMEM((LEVELS, wide, SUB, LANE), f32),
            pltpu.VMEM((wide, SUB, LANE), f32),
            pltpu.VMEM((3,) + plane, f32),
            pltpu.VMEM((2, wide, SUB, LANE), f32),
            pltpu.VMEM((2,) + plane, f32),
            pltpu.VMEM((6,) + plane, f32),
            pltpu.VMEM((2, 3, EXTRA[0], SUB, LANE), f32),
            pltpu.VMEM((STAGES, FOLD, LANE), f32),
            pltpu.VMEM((STAGES, tiles, FOLD, LANE), f32),
            pltpu.VMEM((rows, 2, SUB, LANE), f32),
            pltpu.VMEM((rows, 2, SUB, LANE), f32),
            pltpu.SemaphoreType.DMA((3,)),
            pltpu.SemaphoreType.DMA((3, 2)),
            pltpu.SemaphoreType.DMA((3, 2)),
            pltpu.SemaphoreType.DMA((STAGES, tiles)),
            pltpu.SemaphoreType.DMA((STAGES, tiles)),
            pltpu.SemaphoreType.DMA((chunks,)),
            pltpu.SemaphoreType.DMA((chunks,)),
        ],
        compiler_params=pltpu.CompilerParams(
            collective_id=0, has_side_effects=True, vmem_limit_bytes=48 * 1024 * 1024
        ),
        name="wake_step",
    )(state_in, sea_depth, pressure)


def solution(mesh):
    placed = (P("cuts", None, "tile", None), P("tile", None), P("tile", None))
    return jax.shard_map(
        functools.partial(local, mesh.shape["tile"], mesh.shape["cuts"]),
        mesh=mesh,
        in_specs=placed,
        out_specs=P("cuts", None, "tile", None),
        check_vma=False,
    )
```
